32 devices in a mesh: blk: 8 (over y, x, core), grp: 4 (over z).
Axes of the slice: x: 2, y: 2, z: 4, core: 2. Of those that a mesh axis runs over, the one named last changes fastest.
Arguments:
- query_rows: bfloat16 [16384, 1024], P(('blk', 'grp')), may hold values from -8 to 8
- key_rows: bfloat16 [16384, 1024], P(('blk', 'grp')), may hold values from -8 to 8
- value_rows: bfloat16 [16384, 1024], P(('blk', 'grp')), may hold values from -6 to 6
- tile_lists: int32 [128, 9], P(('blk', 'grp')), may hold values from -1 to 127, as said below
- hilbert_order: int32 [16384], P(('blk', 'grp')), may hold values from 0 to 16383, as said below
Outputs:
- attention_out: bfloat16 [16384, 1024], P(('blk', 'grp'))
The draws below stay inside these ranges and needn't reach their ends.
Inputs may be any that keep to these rules, and one draw needn't show every extreme that they name: `tile_lists`: row r lists the key tiles of query tile r. Slot j for j <= 4 holds r - 2 + j or -1; slot 5 + g holds global tile g, the same in every row, the global tiles lying 32 apart. No tile appears twice in a row, and tile r appears in row r. `hilbert_order`: A permutation that maps each aligned block of 512 positions onto itself.
All inputs are finite; a program needn't handle non-finite values.
Results may differ from the reference program's by a relative error of at most 0.0049.
Values may be sent and summed in bfloat16 or wider, within the bound.
No kernel may reach another device: no remote copies, remote signals or barrier semaphores. Data moves between devices by JAX's collectives and lax.ppermute only.
A program may use at most 64 MiB of HBM per device.

```python
import jax
import jax.numpy as jnp
from jax import lax

LOCAL_HEADS = 8
HEAD_WIDTH = 128
TILE_POINTS = 128
BAND = 2
NG = 4
TOK_DEV = 512
TOKENS = 16384
N_TILES = 128
GSTRIDE = 32
SLOT_COUNT = 9


def draw_query_rows(key, part):
    result = jnp.clip(jax.random.normal(jax.random.fold_in(key, 1), (TOKENS, LOCAL_HEADS * HEAD_WIDTH), jnp.float32), -6.0, 6.0)
    return result.astype(jnp.bfloat16)


def draw_key_rows(key, part):
    result = jnp.clip(jax.random.normal(jax.random.fold_in(key, 2), (TOKENS, LOCAL_HEADS * HEAD_WIDTH), jnp.float32), -6.0, 6.0)
    return result.astype(jnp.bfloat16)


def draw_tile_lists(key, part):
    tile_row = jnp.arange(N_TILES, dtype=jnp.int32)[:, None]
    slot_index = jnp.arange(2 * BAND + 1, dtype=jnp.int32)[None, :]
    target = tile_row - BAND + slot_index
    phase = jax.random.randint(jax.random.fold_in(key, 3), (), 0, GSTRIDE).astype(jnp.int32)
    reach = jax.random.randint(jax.random.fold_in(key, 4), (N_TILES, 1), 1, BAND + 1).astype(jnp.int32)
    inside = (target >= 0) & (target < N_TILES)
    near = jnp.abs(slot_index - BAND) <= reach
    not_global = jnp.mod(target - phase, GSTRIDE) != 0
    band_part = jnp.where(inside & near & not_global, target, -1)
    global_part = jnp.broadcast_to(phase + GSTRIDE * jnp.arange(NG, dtype=jnp.int32)[None, :], (N_TILES, NG))
    return jnp.concatenate([band_part, global_part], axis=1).astype(jnp.int32)


def draw_hilbert_order(key, part):
    blocks = TOKENS // TOK_DEV
    ranking = jax.random.randint(jax.random.fold_in(key, 5), (blocks, TOK_DEV), 0, 1 << 16) * TOK_DEV + jnp.arange(TOK_DEV, dtype=jnp.int32)[None, :]
    order = jnp.argsort(ranking, axis=1, stable=True).astype(jnp.int32) + (jnp.arange(blocks, dtype=jnp.int32) * TOK_DEV)[:, None]
    return order.reshape(-1).astype(jnp.int32)


def steps_of(own_key, dims, pieces, least, top_value):
    loudness, own = 1.0, jax.random.fold_in(own_key, 6)
    for axis_at, shards_of in pieces:
        draws = jnp.exp(jax.random.uniform(jax.random.fold_in(own, axis_at), (shards_of,), jnp.float32, least / len(pieces), top_value / len(pieces)))
        loudness = loudness * jnp.repeat(draws, dims[axis_at] // shards_of).reshape([-1 if axis == axis_at else 1 for axis in range(len(dims))])
    return loudness


def noise(stream_key, dims, width, most, cuts=(), kind=jnp.bfloat16):
    values = jax.random.normal(stream_key, dims, jnp.float32) * width
    if len(cuts) > 0:
        values = steps_of(stream_key, dims, cuts, -0.22, 0.18) * values
    return jnp.clip(values, min=-most, max=most).astype(kind)


def setup_inputs(seed: int = 0) -> dict:
    key_of = jax.random.split(jax.random.key(seed), 6)
    return {
        "query_rows": draw_query_rows(jax.random.fold_in(key_of[5], 71), 0),
        "key_rows": draw_key_rows(jax.random.fold_in(key_of[5], 71), 0),
        "value_rows": noise(key_of[2], (TOKENS, LOCAL_HEADS * HEAD_WIDTH), 1.0, 6.0, ((0, 32),)),
        "tile_lists": draw_tile_lists(jax.random.fold_in(key_of[5], 71), 0),
        "hilbert_order": draw_hilbert_order(jax.random.fold_in(key_of[5], 71), 0),
    }


def reference(query_rows, key_rows, value_rows, tile_lists, hilbert_order):
    q_sorted = query_rows[hilbert_order]
    k_sorted = key_rows[hilbert_order]
    v_sorted = value_rows[hilbert_order]
    score_scale = HEAD_WIDTH ** -0.5
    tiled_keys = k_sorted.reshape(N_TILES, TILE_POINTS, LOCAL_HEADS, HEAD_WIDTH)
    tiled_values = v_sorted.reshape(N_TILES, TILE_POINTS, LOCAL_HEADS, HEAD_WIDTH)
    query_tiles = q_sorted.reshape(N_TILES, TILE_POINTS, LOCAL_HEADS, HEAD_WIDTH)

    def one_tile(inputs):
        queries_here, listed = inputs
        selected_tiles = jnp.maximum(listed, 0).astype(jnp.int32)
        selected_keys = tiled_keys[selected_tiles].reshape(SLOT_COUNT * TILE_POINTS, LOCAL_HEADS, HEAD_WIDTH)
        selected_values = tiled_values[selected_tiles].reshape(SLOT_COUNT * TILE_POINTS, LOCAL_HEADS, HEAD_WIDTH)
        allowed = jnp.repeat(listed >= 0, TILE_POINTS)
        scores = jnp.einsum("qhd,khd->hqk", queries_here.astype(jnp.float32), selected_keys.astype(jnp.float32)) * score_scale
        scores = jnp.where(allowed[None, None, :], scores, -1e30)
        row_peak = jnp.max(scores, axis=-1, keepdims=True)
        exponent = jnp.exp(scores - row_peak)
        weights = (exponent / jnp.sum(exponent, axis=-1, keepdims=True)).astype(jnp.bfloat16)
        attended = jnp.einsum("hqk,khd->qhd", weights.astype(jnp.float32), selected_values.astype(jnp.float32))
        return attended.reshape(TILE_POINTS, LOCAL_HEADS * HEAD_WIDTH).astype(jnp.bfloat16)

    attended = lax.map(one_tile, (query_tiles, tile_lists)).reshape(TOKENS, LOCAL_HEADS * HEAD_WIDTH)
    return jnp.zeros_like(attended).at[hilbert_order].set(attended)
```

```python
import functools

import jax
import jax.numpy as jnp
from jax import lax
from jax.experimental import pallas as pl
from jax.experimental.pallas import tpu as pltpu
from jax.sharding import PartitionSpec as P

LOCAL_HEADS = 8
HEAD_WIDTH = 128
TILE_POINTS = 128
BAND = 2
NG = 4
HALO = BAND * TILE_POINTS
PAIR = 2 * HEAD_WIDTH
MASKED = -1e30
EXP_SCALE = HEAD_WIDTH ** (-0.5) * 1.4426950408889634
VMEM_LIMIT = 48 * 1024 * 1024


def mm(a, b):
    return lax.dot_general(a, b, (((1,), (0,)), ((), ())), preferred_element_type=jnp.float32)


def mm_nt(a, b):
    return lax.dot_general(a, b, (((1,), (1,)), ((), ())), preferred_element_type=jnp.float32)


def pick_rows(order_ref):
    count = order_ref.shape[1]
    order = jnp.bitwise_and(order_ref[...], count - 1)
    column = jnp.transpose(jnp.broadcast_to(order, (128, count)))
    lane = lax.broadcasted_iota(jnp.int32, (count, 128), 1)
    parts = [column == lane + start for start in range(0, count, 128)]
    return jnp.concatenate([p.astype(jnp.float32) for p in parts], axis=1).astype(jnp.bfloat16)


def place_rows(order_ref):
    count = order_ref.shape[1]
    order = jnp.bitwise_and(order_ref[...], count - 1)
    row = lax.broadcasted_iota(jnp.int32, (count, count), 0)
    return (row == order).astype(jnp.float32).astype(jnp.bfloat16)


def bias_rows(lists_ref, query_tile, key_tiles):
    parts = []
    for key_tile in key_tiles:
        slot = key_tile - query_tile + BAND
        if 0 <= slot <= 2 * BAND:
            value = jnp.where(lists_ref[query_tile, slot] >= 0, 0.0, MASKED).astype(jnp.float32)
        else:
            value = jnp.float32(MASKED)
        parts.append(jnp.full((1, TILE_POINTS), value, jnp.float32))
    return jnp.concatenate(parts, axis=1)


def add_bias(scores, lists_ref, query_tiles, key_tiles):
    parts = []
    for at, query_tile in enumerate(query_tiles):
        rows = scores[at * TILE_POINTS : (at + 1) * TILE_POINTS]
        parts.append(rows + bias_rows(lists_ref, query_tile, key_tiles))
    return jnp.concatenate(parts, axis=0)


def sort_kernel(spot_ref, order_ref, k_ref, v_ref, head_ref, tail_ref, *rest):
    pieces, (pick, sorted_kv) = rest[:-2], rest[-2:]

    @pl.when(pl.program_id(0) == 0)
    def _():
        pick[...] = pick_rows(order_ref)

    count = k_ref.shape[0]
    for which, ref in enumerate((k_ref, v_ref)):
        rows = mm(pick[...], ref[...]).astype(jnp.bfloat16)
        sorted_kv[which] = rows
        head_ref[which] = rows[:HALO]
        tail_ref[which] = rows[count - HALO :]
    piece_rows = TILE_POINTS // len(pieces)
    for step, piece_ref in enumerate(pieces):
        number = lax.rem(spot_ref[1] + step, len(pieces))
        start = pl.multiple_of(spot_ref[0] * TILE_POINTS + number * piece_rows, piece_rows)
        piece_ref[...] = sorted_kv[:, pl.ds(start, piece_rows), :]


def local_kernel(lists_ref, order_ref, q_ref, head_ref, tail_ref, qs_ref, acc_ref, ml_ref, pick):
    step = pl.program_id(0)

    @pl.when(step == 0)
    def _():
        pick[...] = pick_rows(order_ref)
        ml_ref[...] = jnp.zeros_like(ml_ref)

    queries = mm(pick[...], q_ref[...]).astype(jnp.bfloat16)
    qs_ref[...] = queries
    tiles = range(q_ref.shape[0] // TILE_POINTS)
    lane = lax.broadcasted_iota(jnp.int32, ml_ref.shape, 1)
    for at in range(PAIR // HEAD_WIDTH):
        cols = slice(at * HEAD_WIDTH, (at + 1) * HEAD_WIDTH)
        keys = jnp.concatenate([head_ref[0, :, cols], tail_ref[0, :, cols]], axis=0)
        values = jnp.concatenate([head_ref[1, :, cols], tail_ref[1, :, cols]], axis=0)
        scores = add_bias(mm_nt(queries[:, cols], keys), lists_ref, tiles, tiles)
        peak = jnp.max(scores, axis=1, keepdims=True)
        weights = jnp.exp2((scores - peak) * EXP_SCALE)
        total = jnp.sum(weights, axis=1, keepdims=True)
        acc_ref[:, cols] = mm(weights.astype(jnp.bfloat16), values)
        head = step * (PAIR // HEAD_WIDTH) + at
        kept = jnp.where(lane == head, peak, ml_ref[...])
        ml_ref[...] = jnp.where(lane == head + LOCAL_HEADS, total, kept)


def finish_kernel(lists_ref, order_ref, qs_ref, acc_ref, ml_ref, low_ref, high_ref, *rest):
    pieces, (out_ref, place) = rest[:-2], rest[-2:]
    step = pl.program_id(0)

    @pl.when(step == 0)
    def _():
        place[...] = place_rows(order_ref)

    count = qs_ref.shape[0]
    tiles_here = count // TILE_POINTS
    lane = lax.broadcasted_iota(jnp.int32, ml_ref.shape, 1)
    results = []
    for at in range(PAIR // HEAD_WIDTH):
        cols = slice(at * HEAD_WIDTH, (at + 1) * HEAD_WIDTH)
        head = step * (PAIR // HEAD_WIDTH) + at
        ml = ml_ref[...]
        old_peak = jnp.sum(jnp.where(lane == head, ml, 0.0), axis=1, keepdims=True)
        old_total = jnp.sum(jnp.where(lane == head + LOCAL_HEADS, ml, 0.0), axis=1, keepdims=True)
        queries = qs_ref[:, cols]
        global_keys = jnp.concatenate([ref[0, :, cols] for ref in pieces], axis=0)
        global_values = jnp.concatenate([ref[1, :, cols] for ref in pieces], axis=0)
        far = mm_nt(queries, global_keys)
        low = add_bias(
            mm_nt(queries[:HALO], low_ref[0, :, cols]), lists_ref, range(BAND), range(-BAND, 0)
        )
        high = add_bias(
            mm_nt(queries[count - HALO :], high_ref[0, :, cols]),
            lists_ref,
            range(tiles_here - BAND, tiles_here),
            range(tiles_here, tiles_here + BAND),
        )
        near_peak = jnp.concatenate(
            [jnp.max(low, axis=1, keepdims=True), jnp.max(high, axis=1, keepdims=True)], axis=0
        )
        peak = jnp.maximum(jnp.maximum(old_peak, near_peak), jnp.max(far, axis=1, keepdims=True))
        shrink = jnp.exp2((old_peak - peak) * EXP_SCALE)
        far = jnp.exp2((far - peak) * EXP_SCALE)
        low = jnp.exp2((low - peak[:HALO]) * EXP_SCALE)
        high = jnp.exp2((high - peak[count - HALO :]) * EXP_SCALE)
        near_total = jnp.concatenate(
            [jnp.sum(low, axis=1, keepdims=True), jnp.sum(high, axis=1, keepdims=True)], axis=0
        )
        total = old_total * shrink + near_total + jnp.sum(far, axis=1, keepdims=True)
        near_sum = jnp.concatenate(
            [
                mm(low.astype(jnp.bfloat16), low_ref[1, :, cols]),
                mm(high.astype(jnp.bfloat16), high_ref[1, :, cols]),
            ],
            axis=0,
        )
        summed = acc_ref[:, cols] * shrink + near_sum + mm(far.astype(jnp.bfloat16), global_values)
        results.append((summed / total).astype(jnp.bfloat16))
    attended = jnp.concatenate(results, axis=1)
    out_ref[...] = mm(place[...], attended).astype(jnp.bfloat16)


def column_block(*leading):
    zeros = (0,) * len(leading)
    return pl.BlockSpec((*leading, PAIR), lambda i: (*zeros, i))


def whole_block(*shape):
    return pl.BlockSpec(shape, lambda i: (0,) * len(shape))


SCALARS = pl.BlockSpec(memory_space=pltpu.SMEM)


def spread_along(piece, axis, root):
    count = lax.axis_size(axis)
    at = lax.axis_index(axis)
    middle = count // 2
    for i in range(middle - 1):
        got = lax.ppermute(piece, axis, [(i, i + 1), (count - 1 - i, count - 2 - i)])
        take = ((at == i + 1) & (root <= i)) | ((at == count - 2 - i) & (root >= count - 1 - i))
        piece = jnp.where(take, got, piece)
    got = lax.ppermute(piece, axis, [(middle - 1, middle), (middle, middle - 1)])
    take = ((at == middle) & (root < middle)) | ((at == middle - 1) & (root >= middle))
    piece = jnp.where(take, got, piece)
    for i in range(middle - 1, 0, -1):
        got = lax.ppermute(piece, axis, [(i, i - 1), (count - 1 - i, count - i)])
        take = ((at == i - 1) & (root >= i)) | ((at == count - i) & (root <= count - 1 - i))
        piece = jnp.where(take, got, piece)
    return piece


def body(query_rows, key_rows, value_rows, tile_lists, hilbert_order):
    row_count, feature_count = query_rows.shape
    tiles_here = row_count // TILE_POINTS
    blk_count, grp_count = lax.axis_size("blk"), lax.axis_size("grp")
    part = blk_count // NG
    steps = feature_count // PAIR
    grid = (steps,)
    params = pltpu.CompilerParams(vmem_limit_bytes=VMEM_LIMIT)
    bf16 = functools.partial(jax.ShapeDtypeStruct, dtype=jnp.bfloat16)
    f32 = functools.partial(jax.ShapeDtypeStruct, dtype=jnp.float32)

    order = hilbert_order.reshape(1, row_count)
    tile_id = tile_lists[0, 2 * BAND + 1] % (tiles_here * blk_count * grp_count // NG)
    owner, owner_tile = tile_id // tiles_here, tile_id % tiles_here
    owner_blk, owner_grp = owner // grp_count, owner % grp_count
    my_part = lax.axis_index("blk") % part
    spot = jnp.stack([owner_tile, my_part]).astype(jnp.int32)

    piece_rows = TILE_POINTS // part
    head, tail, *pieces = pl.pallas_call(
        sort_kernel,
        grid=grid,
        in_specs=[
            SCALARS,
            whole_block(1, row_count),
            column_block(row_count),
            column_block(row_count),
        ],
        out_specs=[column_block(2, HALO)] * 2 + [column_block(2, piece_rows)] * part,
        out_shape=[bf16((2, HALO, feature_count))] * 2
        + [bf16((2, piece_rows, feature_count))] * part,
        scratch_shapes=[
            pltpu.VMEM((row_count, row_count), jnp.bfloat16),
            pltpu.VMEM((2, row_count, PAIR), jnp.bfloat16),
        ],
        compiler_params=params,
        name="sort_keys_values",
    )(spot, order, key_rows, value_rows)

    piece = pieces[0]
    for step in range(1, part):
        pairs = [(i, i // part * part + (i + step) % part) for i in range(blk_count)]
        got = lax.ppermute(pieces[step], "blk", pairs)
        piece = jnp.where((my_part - step) % part == owner_blk, got, piece)
    piece = spread_along(piece, "grp", owner_grp)

    axes = ("blk", "grp")
    count = blk_count * grp_count
    forward = [(i, i + 1) for i in range(count - 1)]
    low = lax.ppermute(tail, axes, forward)
    high = lax.ppermute(head, axes, [(target, source) for source, target in forward])

    gathered = [piece]
    for quarter in range(1, NG):
        pairs = [(i, (i // part ^ quarter) * part + i % part) for i in range(blk_count)]
        gathered.append(lax.ppermute(piece, "blk", pairs))
    quarters = jnp.concatenate(gathered, axis=1)
    global_pieces = [quarters]
    for step in range(1, part):
        pairs = [(i, i // part * part + (i + step) % part) for i in range(blk_count)]
        global_pieces.append(lax.ppermute(quarters, "blk", pairs))

    queries, summed, peaks = pl.pallas_call(
        local_kernel,
        grid=grid,
        in_specs=[
            SCALARS,
            whole_block(1, row_count),
            column_block(row_count),
            column_block(2, HALO),
            column_block(2, HALO),
        ],
        out_specs=[column_block(row_count), column_block(row_count), whole_block(row_count, 128)],
        out_shape=[
            bf16((row_count, feature_count)),
            f32((row_count, feature_count)),
            f32((row_count, 128)),
        ],
        scratch_shapes=[pltpu.VMEM((row_count, row_count), jnp.bfloat16)],
        compiler_params=params,
        name="attend_own",
    )(tile_lists, order, query_rows, head, tail)

    return pl.pallas_call(
        finish_kernel,
        grid=grid,
        in_specs=[
            SCALARS,
            whole_block(1, row_count),
            column_block(row_count),
            column_block(row_count),
            whole_block(row_count, 128),
            column_block(2, HALO),
            column_block(2, HALO),
        ]
        + [column_block(2, NG * piece_rows)] * part,
        out_specs=column_block(row_count),
        out_shape=bf16((row_count, feature_count)),
        scratch_shapes=[pltpu.VMEM((row_count, row_count), jnp.bfloat16)],
        compiler_params=params,
        name="attend_rest",
    )(tile_lists, order, queries, summed, peaks, low, high, *global_pieces)


def solution(mesh):
    rows = P(("blk", "grp"), None)
    in_specs = (rows, rows, rows, rows, P(("blk", "grp")))
    return jax.shard_map(body, mesh=mesh, in_specs=in_specs, out_specs=rows, check_vma=False)
```

```python
import functools

import jax
import jax.numpy as jnp
from jax import lax
from jax.experimental import pallas as pl
from jax.experimental.pallas import tpu as pltpu
from jax.sharding import PartitionSpec as P

LOCAL_HEADS = 8
HEAD_WIDTH = 128
TILE_POINTS = 128
BAND = 2
NG = 4
HALO = BAND * TILE_POINTS
PAIR_HEADS = 4
PAIR = PAIR_HEADS * HEAD_WIDTH
STATE_ROWS = 8
MASKED = -1e30
EXP_SCALE = HEAD_WIDTH ** (-0.5) * 1.4426950408889634
VMEM_LIMIT = 16 * 1024 * 1024


def mm(a, b):
    return lax.dot_general(a, b, (((1,), (0,)), ((), ())), preferred_element_type=jnp.float32)


def mm_tn(a, b):
    return lax.dot_general(a, b, (((0,), (0,)), ((), ())), preferred_element_type=jnp.float32)


def mm_nt(a, b):
    return lax.dot_general(a, b, (((1,), (1,)), ((), ())), preferred_element_type=jnp.float32)


def pick_rows(order):
    count = order.shape[1]
    column = jnp.transpose(jnp.broadcast_to(order, (128, count)))
    lane = lax.broadcasted_iota(jnp.int32, (count, 128), 1)
    parts = [column == lane + start for start in range(0, count, 128)]
    return jnp.concatenate([p.astype(jnp.float32) for p in parts], axis=1).astype(jnp.bfloat16)


def place_rows(order):
    count = order.shape[1]
    row = lax.broadcasted_iota(jnp.int32, (count, count), 0)
    return (row == order).astype(jnp.float32).astype(jnp.bfloat16)


def local_order(order_ref):
    return jnp.bitwise_and(order_ref[...], order_ref.shape[1] - 1)


def add_bias(scores, lists_ref, first_query, first_key):
    parts = []
    for at in range(scores.shape[0] // TILE_POINTS):
        bias = []
        for query in range(scores.shape[1] // TILE_POINTS):
            slot = first_key + at - first_query - query + BAND
            listed = lists_ref[first_query + query, jnp.clip(slot, 0, 2 * BAND)] >= 0
            admitted = listed & (slot >= 0) & (slot <= 2 * BAND)
            value = jnp.where(admitted, 0.0, MASKED).astype(jnp.float32)
            bias.append(jnp.full((1, TILE_POINTS), value, jnp.float32))
        rows = scores[at * TILE_POINTS : (at + 1) * TILE_POINTS]
        parts.append(rows + jnp.concatenate(bias, axis=1))
    return jnp.concatenate(parts, axis=0)


def exp_of(scores, peak):
    return jnp.exp2((scores - peak) * EXP_SCALE)


def peak_of(scores):
    return jnp.max(scores, axis=0, keepdims=True)


def total_of(weights):
    return jnp.sum(weights, axis=0, keepdims=True)


def columns_of(head):
    return slice(head * HEAD_WIDTH, (head + 1) * HEAD_WIDTH)


def in_lower_half():
    return lax.axis_index("grp") < lax.axis_size("grp") // 2


def sort_kernel(lists_hbm, order_hbm, k_hbm, v_hbm, kv_hbm, outward, inward, first_out, second_out, *rest):
    pieces = rest[:-7]
    lists_ref, order_ref, unsorted, sorted_kv, arrived, left, small = rest[-7:]
    count, width = k_hbm.shape
    order_copy = pltpu.make_async_copy(order_hbm, order_ref, small.at[0])
    lists_copy = pltpu.make_async_copy(lists_hbm, lists_ref, small.at[1])
    order_copy.start()
    lists_copy.start()
    copies = []
    for which, ref in enumerate((k_hbm, v_hbm)):
        for start in range(0, count, TILE_POINTS):
            rows = pl.ds(start, TILE_POINTS)
            done = arrived.at[which, start // TILE_POINTS]
            copies.append(pltpu.make_async_copy(ref.at[rows], unsorted.at[which, rows], done))
    for copy in copies:
        copy.start()
    order_copy.wait()
    pick = pick_rows(local_order(order_ref))
    lists_copy.wait()
    tile = lax.rem(lists_ref[0, 2 * BAND + 1], count // TILE_POINTS)
    mine = lax.rem(lax.axis_index("blk"), len(pieces))
    piece_rows = TILE_POINTS // len(pieces)
    low, high = 0, count - HALO
    outward_first = lax.rem(lax.axis_index("blk"), 2) == 0
    out_start = jnp.where(in_lower_half(), low, high)
    in_start = jnp.where(in_lower_half(), high, low)
    out_rows = pl.ds(pl.multiple_of(out_start, HALO), HALO)
    in_rows = pl.ds(pl.multiple_of(in_start, HALO), HALO)
    first_rows = pl.ds(pl.multiple_of(jnp.where(outward_first, out_start, in_start), HALO), HALO)
    second_rows = pl.ds(pl.multiple_of(jnp.where(outward_first, in_start, out_start), HALO), HALO)
    leaving = []
    for which in range(2):
        for copy in copies[which * len(copies) // 2 : (which + 1) * len(copies) // 2]:
            copy.wait()
        for start in range(0, width, PAIR):
            cols = pl.ds(start, PAIR)
            rows = mm(pick, unsorted[which, :, start : start + PAIR]).astype(jnp.bfloat16)
            sorted_kv[which, :, start : start + PAIR] = rows
            targets = [
                (slice(None), kv_hbm.at[which, :, cols]),
                (out_rows, outward.at[which, :, cols]),
                (in_rows, inward.at[which, :, cols]),
                (first_rows, first_out.at[which, :, cols]),
                (second_rows, second_out.at[which, :, cols]),
            ]
            for step, piece_ref in enumerate(pieces):
                first = tile * TILE_POINTS + lax.rem(mine + step, len(pieces)) * piece_rows
                first = pl.multiple_of(first, piece_rows)
                targets.append((pl.ds(first, piece_rows), piece_ref.at[which, :, cols]))
            for number, (taken, target) in enumerate(targets):
                done = left.at[which, start // PAIR, number]
                copy = pltpu.make_async_copy(sorted_kv.at[which, taken, cols], target, done)
                copy.start()
                leaving.append(copy)
    for copy in leaving:
        copy.wait()


def select_kernel(rule, lists_ref, got_ref, held_ref, out_ref):
    out_ref[...] = jnp.where(rule(lists_ref[0, 2 * BAND + 1]), got_ref[...], held_ref[...])


def query_kernel(order_ref, q_ref, qs_ref, place_ref, pick):
    @pl.when(pl.program_id(0) == 0)
    def _():
        order = local_order(order_ref)
        place_ref[...] = place_rows(order)
        pick[...] = pick_rows(order)

    qs_ref[...] = mm(pick[...], q_ref[...]).astype(jnp.bfloat16)


def own_kernel(lists_ref, qs_ref, kv_ref, acc_ref, ml_ref):
    for at in range(PAIR_HEADS):
        cols = columns_of(at)
        scores = add_bias(mm_nt(kv_ref[0, :, cols], qs_ref[:, cols]), lists_ref, 0, 0)
        peak = peak_of(scores)
        weights = exp_of(scores, peak)
        ml_ref[at : at + 1] = peak
        ml_ref[PAIR_HEADS + at : PAIR_HEADS + at + 1] = total_of(weights)
        acc_ref[cols] = mm_tn(kv_ref[1, :, cols], weights.astype(jnp.bfloat16))


def halo_place(is_low, count):
    tiles = count // TILE_POINTS
    start = pl.multiple_of(jnp.where(is_low, 0, count - HALO), HALO)
    return start, jnp.where(is_low, 0, tiles - BAND), jnp.where(is_low, -BAND, tiles)


def take_keys(old, scores, values, summed):
    old_peak, old_total = old
    peak = jnp.maximum(old_peak, peak_of(scores))
    shrink = exp_of(old_peak, peak)
    weights = exp_of(scores, peak)
    total = old_total * shrink + total_of(weights)
    return peak, total, summed * shrink + mm_tn(values, weights.astype(jnp.bfloat16))


def at_middle():
    here, middle = lax.axis_index("grp"), lax.axis_size("grp") // 2
    return (here == middle) | (here == middle - 1)


def meets_early():
    return at_middle() == (lax.rem(lax.axis_index("blk"), 2) == 1)


def near_kernel(lists_ref, qs_ref, near_kv, acc_ref, ml_ref, new_acc_ref, new_ml_ref):
    new_acc_ref[...] = acc_ref[...]
    new_ml_ref[...] = ml_ref[...]

    @pl.when(meets_early())
    def _():
        start, first_query, first_key = halo_place(jnp.logical_not(in_lower_half()), qs_ref.shape[0])
        met = pl.ds(start, HALO)
        for at in range(PAIR_HEADS):
            cols = columns_of(at)
            scores = mm_nt(near_kv[0, :, cols], qs_ref[met, cols])
            scores = add_bias(scores, lists_ref, first_query, first_key)
            old = ml_ref[at : at + 1, met], ml_ref[PAIR_HEADS + at : PAIR_HEADS + at + 1, met]
            peak, total, summed = take_keys(old, scores, near_kv[1, :, cols], acc_ref[cols, met])
            new_acc_ref[cols, met] = summed
            new_ml_ref[at : at + 1, met] = peak
            new_ml_ref[PAIR_HEADS + at : PAIR_HEADS + at + 1, met] = total


def global_kernel(lists_ref, qs_ref, acc_ref, ml_ref, *rest):
    pieces, (new_acc_ref, new_ml_ref) = rest[:-2], rest[-2:]
    for at in range(PAIR_HEADS):
        cols = columns_of(at)
        old = ml_ref[at : at + 1], ml_ref[PAIR_HEADS + at : PAIR_HEADS + at + 1]
        keys = jnp.concatenate([ref[0, :, cols] for ref in pieces], axis=0)
        values = jnp.concatenate([ref[1, :, cols] for ref in pieces], axis=0)
        peak, total, summed = take_keys(old, mm_nt(keys, qs_ref[:, cols]), values, acc_ref[cols])
        new_acc_ref[cols] = summed
        new_ml_ref[at : at + 1] = peak
        new_ml_ref[PAIR_HEADS + at : PAIR_HEADS + at + 1] = total


def finish_kernel(lists_ref, place_ref, qs_ref, acc_ref, ml_ref, *rest):
    next_kv, late_kv, even_kv, odd_kv, out_ref, attended, halos, arrived = rest
    count = qs_ref.shape[0]
    here, end = lax.axis_index("grp"), lax.axis_size("grp") - 1
    at_end = (here == 0) | (here == end)
    even_wrap = (lax.rem(lax.axis_index("blk"), 2) == 0) == (here == end)
    sources = (
        (jnp.logical_not(at_end), 0, next_kv),
        (at_end & even_wrap, 0, even_kv),
        (at_end & jnp.logical_not(even_wrap), 0, odd_kv),
        (jnp.logical_not(meets_early()), 1, late_kv),
    )
    step = pl.program_id(0)

    @pl.when(step == 0)
    def _():
        copies = []
        for chosen, side, source in sources:
            pieces = [
                pltpu.make_async_copy(source.at[w], halos.at[side, w], arrived.at[side, w]) for w in range(2)
            ]
            copies.append((chosen, pieces))

            @pl.when(chosen)
            def _():
                for copy in pieces:
                    copy.start()

        for chosen, pieces in copies:

            @pl.when(chosen)
            def _():
                for copy in pieces:
                    copy.wait()

    def add_halo(side, is_low):
        start, first_query, first_key = halo_place(is_low, count)
        met = pl.ds(start, HALO)
        for at in range(PAIR_HEADS):
            cols = columns_of(at)
            here_cols = pl.ds(pl.multiple_of(step * PAIR + at * HEAD_WIDTH, HEAD_WIDTH), HEAD_WIDTH)
            scores = mm_nt(halos[side, 0, :, here_cols], qs_ref[met, cols])
            scores = add_bias(scores, lists_ref, first_query, first_key)
            old = ml_ref[at : at + 1, met], ml_ref[PAIR_HEADS + at : PAIR_HEADS + at + 1, met]
            _, total, summed = take_keys(old, scores, halos[side, 1, :, here_cols], acc_ref[cols, met])
            attended[cols, met] = (summed / total).astype(jnp.bfloat16)

    add_halo(0, in_lower_half())

    @pl.when(jnp.logical_not(meets_early()))
    def _():
        add_halo(1, jnp.logical_not(in_lower_half()))

    @pl.when(meets_early())
    def _():
        start, _, _ = halo_place(jnp.logical_not(in_lower_half()), count)
        left = pl.ds(start, HALO)
        for at in range(PAIR_HEADS):
            cols = columns_of(at)
            total = ml_ref[PAIR_HEADS + at : PAIR_HEADS + at + 1, left]
            attended[cols, left] = (acc_ref[cols, left] / total).astype(jnp.bfloat16)

    out_ref[...] = mm_nt(place_ref[...], attended[...]).astype(jnp.bfloat16)


def join_kernel(first, second, joined):
    rows = first.shape[1]
    joined[:, :rows] = first[...]
    joined[:, rows:] = second[...]


SMEM = pl.BlockSpec(memory_space=pltpu.SMEM)
VMEM = pl.BlockSpec(memory_space=pltpu.VMEM)
HBM = pl.BlockSpec(memory_space=pltpu.HBM)
ANY = pl.BlockSpec(memory_space=pl.ANY)
SORT_LIMIT = VMEM_LIMIT
LONG = 20000000000


def column_block(*leading):
    zeros = (0,) * len(leading)
    return pl.BlockSpec((*leading, PAIR), lambda i: (*zeros, i))


def row_block(rows, width):
    return pl.BlockSpec((rows, width), lambda i: (i, 0))


def whole_block(*shape):
    return pl.BlockSpec(shape, lambda i: (0,) * len(shape))


def spread_rounds(axis):
    count = lax.axis_size(axis)
    middle = count // 2

    def round_of(pairs, low_end, high_start):
        (_, upper), (_, lower) = pairs

        def rule(root):
            at = lax.axis_index(axis)
            return ((at == upper) & (root < low_end)) | ((at == lower) & (root >= high_start))

        return pairs, rule

    rounds = []
    for i in range(middle - 1):
        rounds.append(round_of([(i, i + 1), (count - 1 - i, count - 2 - i)], i + 1, count - 1 - i))
    rounds.append(round_of([(middle - 1, middle), (middle, middle - 1)], middle, middle))
    for i in range(middle - 1, 0, -1):
        rounds.append(round_of([(count - 1 - i, count - i), (i, i - 1)], count - i, i))
    return rounds


def body(query_rows, key_rows, value_rows, tile_lists, hilbert_order):
    row_count, feature_count = query_rows.shape
    tiles_here = row_count // TILE_POINTS
    blk_count, grp_count = lax.axis_size("blk"), lax.axis_size("grp")
    part = blk_count // NG
    bf16 = functools.partial(jax.ShapeDtypeStruct, dtype=jnp.bfloat16)
    f32 = functools.partial(jax.ShapeDtypeStruct, dtype=jnp.float32)

    def in_hbm(*arrays):
        return [pltpu.with_memory_space_constraint(array, pltpu.HBM) for array in arrays]

    def call(kernel, name, ins, outs, out_shape, scratch=(), cost=None, grid=(), limit=VMEM_LIMIT):
        return pl.pallas_call(
            kernel,
            grid=grid,
            in_specs=ins,
            out_specs=outs,
            out_shape=out_shape,
            scratch_shapes=scratch,
            cost_estimate=cost,
            compiler_params=pltpu.CompilerParams(vmem_limit_bytes=limit),
            name=name,
        )

    order = hilbert_order.reshape(1, row_count)
    piece_rows = TILE_POINTS // part
    halo = bf16((2, HALO, feature_count))
    kv, outward, inward, first_out, second_out, *pieces = call(
        sort_kernel,
        "sort_keys_values",
        [HBM] * 4,
        [ANY] * (5 + part),
        [bf16((2, row_count, feature_count)), *[halo] * 4]
        + [bf16((2, piece_rows, feature_count))] * part,
        [
            pltpu.SMEM(tile_lists.shape, jnp.int32),
            pltpu.VMEM((1, row_count), jnp.int32),
            pltpu.VMEM((2, row_count, feature_count), jnp.bfloat16),
            pltpu.VMEM((2, row_count, feature_count), jnp.bfloat16),
            pltpu.SemaphoreType.DMA((2, tiles_here)),
            pltpu.SemaphoreType.DMA((2, feature_count // PAIR, 5 + part)),
            pltpu.SemaphoreType.DMA((2,)),
        ],
        limit=SORT_LIMIT,
    )(tile_lists, order, *in_hbm(key_rows, value_rows))

    def owner_of(tile_id):
        owner = lax.div(lax.rem(tile_id, tiles_here * blk_count * grp_count // NG), tiles_here)
        return lax.div(owner, grp_count), lax.rem(owner, grp_count)

    def select(rule, got, held, flops=1):
        return call(
            functools.partial(select_kernel, rule),
            "select_piece",
            [SMEM] + [VMEM] * 2,
            VMEM,
            bf16(held.shape),
            cost=pl.CostEstimate(flops=flops, bytes_accessed=flops, transcendentals=0),
        )(tile_lists, got, held)

    middle = grp_count // 2
    away = [(i, i - 1) for i in range(1, middle)] + [(i, i + 1) for i in range(middle, grp_count - 1)]
    towards = [(target, source) for source, target in away]
    across = [(middle - 1, middle), (middle, middle - 1)]

    def exchange(turn):
        links = []
        for run in range(blk_count):
            chosen = (away, across)[(run + turn) % 2]
            links += [(run * grp_count + i, run * grp_count + j) for i, j in chosen]
        return links

    wraps = [[], []]
    for run in range(1, blk_count):
        first = run * grp_count
        wraps[(run + 1) % 2] += [(first - 1, first), (first, first - 1)]
    tie = lax.optimization_barrier
    rounds = spread_rounds("grp")
    inner = middle - 1
    listed = tile_lists[0, 2 * BAND + 1] >= 0

    def stage(run, *operands):
        shapes = jax.eval_shape(run, *operands)
        skip = lambda *_: jax.tree.map(lambda leaf: jnp.zeros(leaf.shape, leaf.dtype), shapes)
        return lax.cond(listed, run, skip, *operands)

    def send(piece, some):
        for pairs, rule in some[:-1]:
            piece = take(rule, lax.ppermute(piece, "grp", pairs), piece)
        return piece, lax.ppermute(piece, "grp", some[-1][0])

    def take(rule, got, piece, **cost):
        return select(lambda tile_id: rule(owner_of(tile_id)[1]), got, piece, **cost)

    grid = (feature_count // PAIR,)
    idle = pl.CostEstimate(flops=1, bytes_accessed=1, transcendentals=0)
    busy = pl.CostEstimate(flops=LONG, bytes_accessed=LONG, transcendentals=0)
    queries_block = column_block(row_count)
    state_blocks = [row_block(PAIR, row_count), row_block(STATE_ROWS, row_count)]
    state_shapes = [f32((feature_count, row_count)), f32((grid[0] * STATE_ROWS, row_count))]
    inward_rounds, across_round, outward_rounds = rounds[:inner], rounds[inner], rounds[inner + 1 :]

    def inward_stage(piece):
        queries, place = call(
            query_kernel,
            "sort_queries",
            [whole_block(1, row_count), queries_block],
            [queries_block, whole_block(row_count, row_count)],
            [bf16((row_count, feature_count)), bf16((row_count, row_count))],
            [pltpu.VMEM((row_count, row_count), jnp.bfloat16)],
            cost=busy,
            grid=grid,
        )(order, query_rows)
        return *send(piece, inward_rounds), queries, place

    def across_stage(piece, kv, queries):
        own = call(
            own_kernel,
            "attend_own",
            [SMEM, queries_block, column_block(2, row_count)],
            state_blocks,
            state_shapes,
            cost=busy,
            grid=grid,
        )(tile_lists, queries, kv)
        piece, got = send(piece, [across_round])
        return take(across_round[1], got, piece), own

    def outward_stage(piece, outward, second_out, queries, own, near_kv):
        late_kv = lax.ppermute(second_out, ("blk", "grp"), exchange(1))
        own = call(
            near_kernel,
            "attend_near",
            [SMEM, queries_block, column_block(2, HALO)] + state_blocks,
            state_blocks,
            state_shapes,
            cost=busy,
            grid=grid,
        )(tile_lists, queries, near_kv, *own)
        piece, got = send(piece, outward_rounds)
        got, outward = tie((got, outward))
        even_kv = lax.ppermute(outward, ("blk", "grp"), wraps[0])
        piece = take(outward_rounds[-1][1], got, piece, flops=LONG)
        states, odd_kv = stage(plane_stage, piece, outward, queries, own)
        return states, late_kv, even_kv, odd_kv

    def plane_stage(piece, outward, queries, own):
        for step in range(2):
            turns = [1 if i % part % 2 == step else 2 for i in range(blk_count)]
            links = [(i, (i // part ^ turn) * part + i % part) for i, turn in enumerate(turns)]
            got = lax.ppermute(piece, "blk", links)
            if step == 1:
                got, outward = tie((got, outward))
                odd_kv = lax.ppermute(outward, ("blk", "grp"), wraps[1])
            rows = 2 * piece.shape[1]
            joined = bf16((2, rows, feature_count))
            cost = (idle, busy)[step]
            piece = call(join_kernel, "join_pieces", [VMEM] * 2, VMEM, joined, cost=cost)(piece, got)
        return stage(global_stage, piece, queries, own), odd_kv

    def global_stage(quarters, queries, own):
        pieces = [quarters]
        for step in range(1, part):
            pairs = [(i, i // part * part + (i + step) % part) for i in range(blk_count)]
            pieces.append(lax.ppermute(quarters, "blk", pairs))
        return call(
            global_kernel,
            "attend_global",
            [SMEM, queries_block] + state_blocks + [column_block(2, NG * piece_rows)] * part,
            state_blocks,
            state_shapes,
            cost=idle,
            grid=grid,
        )(tile_lists, queries, *own, *pieces)

    near_kv = lax.ppermute(first_out, ("blk", "grp"), exchange(0))
    piece = pieces[0]
    for step in range(1, part):
        pairs = [(i, i // part * part + (i + step) % part) for i in range(blk_count)]
        got = lax.ppermute(pieces[step], "blk", pairs)

        def from_owner(tile_id, step=step):
            return lax.rem(lax.axis_index("blk") + part - step, part) == owner_of(tile_id)[0]

        piece = select(from_owner, got, piece, flops=LONG)
    piece, got, queries, place = stage(inward_stage, piece)
    got, inward = tie((got, inward))
    next_kv = lax.ppermute(inward, "grp", towards)
    piece = take(inward_rounds[-1][1], got, piece)
    piece, own = stage(across_stage, piece, kv, queries)
    piece, near_kv = tie((piece, near_kv))
    states, late_kv, even_kv, odd_kv = stage(outward_stage, piece, outward, second_out, queries, own, near_kv)
    return call(
        finish_kernel,
        "attend_last",
        [SMEM, whole_block(row_count, row_count), queries_block] + state_blocks + [ANY] * 4,
        queries_block,
        bf16((row_count, feature_count)),
        [
            pltpu.VMEM((PAIR, row_count), jnp.bfloat16),
            pltpu.VMEM((2, 2, HALO, feature_count), jnp.bfloat16),
            pltpu.SemaphoreType.DMA((2, 2)),
        ],
        grid=grid,
    )(tile_lists, place, queries, *states, next_kv, late_kv, even_kv, odd_kv)


def solution(mesh):
    rows = P(("blk", "grp"), None)
    in_specs = (rows, rows, rows, rows, P(("blk", "grp")))
    return jax.shard_map(body, mesh=mesh, in_specs=in_specs, out_specs=rows, check_vma=False)
```

```python
import functools

import jax
import jax.numpy as jnp
from jax import lax
from jax.experimental import pallas as pl
from jax.experimental.pallas import tpu as pltpu
from jax.sharding import PartitionSpec as P

LOCAL_HEADS = 8
HEAD_WIDTH = 128
TILE_POINTS = 128
BAND = 2
NG = 4
HALO = BAND * TILE_POINTS
PAIR_HEADS = 4
PAIR = PAIR_HEADS * HEAD_WIDTH
STATE_ROWS = 2 * PAIR_HEADS
MASKED = -1e30
EXP_SCALE = HEAD_WIDTH ** (-0.5) * 1.4426950408889634
VMEM_LIMIT = 16 * 1024 * 1024


def mm(a, b):
    return lax.dot_general(a, b, (((1,), (0,)), ((), ())), preferred_element_type=jnp.float32)


def mm_tn(a, b):
    return lax.dot_general(a, b, (((0,), (0,)), ((), ())), preferred_element_type=jnp.float32)


def mm_nt(a, b):
    return lax.dot_general(a, b, (((1,), (1,)), ((), ())), preferred_element_type=jnp.float32)


def pick_rows(order):
    count = order.shape[1]
    column = jnp.transpose(jnp.broadcast_to(order, (128, count)))
    lane = lax.broadcasted_iota(jnp.int32, (count, 128), 1)
    parts = [column == lane + start for start in range(0, count, 128)]
    return jnp.concatenate([p.astype(jnp.float32) for p in parts], axis=1).astype(jnp.bfloat16)


def place_rows(order):
    count = order.shape[1]
    row = lax.broadcasted_iota(jnp.int32, (count, count), 0)
    return (row == order).astype(jnp.float32).astype(jnp.bfloat16)


def local_order(order_ref):
    return jnp.bitwise_and(order_ref[...], order_ref.shape[1] - 1)


def bias_rows(lists_ref, queries, keys, first_query, first_key):
    rows = []
    for at in range(keys // TILE_POINTS):
        bias = []
        for query in range(queries // TILE_POINTS):
            slot = first_key + at - first_query - query + BAND
            listed = lists_ref[first_query + query, jnp.clip(slot, 0, 2 * BAND)] >= 0
            admitted = listed & (slot >= 0) & (slot <= 2 * BAND)
            value = jnp.where(admitted, 0.0, MASKED).astype(jnp.float32)
            bias.append(jnp.full((1, TILE_POINTS), value, jnp.float32))
        rows.append(jnp.concatenate(bias, axis=1))
    return rows


def add_bias(scores, rows):
    tiles = [scores[at * TILE_POINTS : (at + 1) * TILE_POINTS] + row for at, row in enumerate(rows)]
    return jnp.concatenate(tiles, axis=0)


def exp_of(scores, peak):
    return jnp.exp2((scores - peak) * EXP_SCALE)


def peak_of(scores):
    return jnp.max(scores, axis=0, keepdims=True)


def total_of(weights):
    return jnp.sum(weights, axis=0, keepdims=True)


def columns_of(head):
    return slice(head * HEAD_WIDTH, (head + 1) * HEAD_WIDTH)


def in_lower_half():
    return lax.axis_index("grp") < lax.axis_size("grp") // 2


def at_middle():
    here, middle = lax.axis_index("grp"), lax.axis_size("grp") // 2
    return (here == middle) | (here == middle - 1)


def meets_early():
    return in_lower_half() == (lax.rem(lax.axis_index("blk"), 2) == 1)


def sort_kernel(lists_hbm, order_hbm, k_hbm, v_hbm, kv_hbm, outward, inward, first_out, second_out, *rest):
    pieces = rest[:-7]
    lists_ref, order_ref, unsorted, sorted_kv, arrived, left, small = rest[-7:]
    count, width = k_hbm.shape
    order_copy = pltpu.make_async_copy(order_hbm, order_ref, small.at[0])
    lists_copy = pltpu.make_async_copy(lists_hbm, lists_ref, small.at[1])
    order_copy.start()
    lists_copy.start()
    copies = []
    for which, ref in enumerate((k_hbm, v_hbm)):
        for start in range(0, count, TILE_POINTS):
            rows = pl.ds(start, TILE_POINTS)
            done = arrived.at[which, start // TILE_POINTS]
            copies.append(pltpu.make_async_copy(ref.at[rows], unsorted.at[which, rows], done))
    for copy in copies:
        copy.start()
    order_copy.wait()
    pick = pick_rows(local_order(order_ref))
    lists_copy.wait()
    tile = lax.rem(lists_ref[0, 2 * BAND + 1], count // TILE_POINTS)
    mine = lax.rem(lax.axis_index("blk"), len(pieces))
    piece_rows = TILE_POINTS // len(pieces)
    low, high = 0, count - HALO
    out_start = jnp.where(in_lower_half(), low, high)
    in_start = jnp.where(in_lower_half(), high, low)
    first_start = jnp.where(at_middle() & jnp.logical_not(meets_early()), in_start, out_start)
    second_start = jnp.where(at_middle() & meets_early(), in_start, out_start)
    starts = (out_start, in_start, first_start, second_start)
    out_rows, in_rows, first_rows, second_rows = [pl.ds(pl.multiple_of(start, HALO), HALO) for start in starts]
    leaving = []
    for which in range(2):
        for copy in copies[which * len(copies) // 2 : (which + 1) * len(copies) // 2]:
            copy.wait()
        for start in range(0, width, PAIR):
            cols = pl.ds(start, PAIR)
            rows = mm(pick, unsorted[which, :, start : start + PAIR]).astype(jnp.bfloat16)
            sorted_kv[which, :, start : start + PAIR] = rows
            targets = [
                (slice(None), kv_hbm.at[which, :, cols]),
                (out_rows, outward.at[which, :, cols]),
                (in_rows, inward.at[which, :, cols]),
                (first_rows, first_out.at[which, :, cols]),
                (second_rows, second_out.at[which, :, cols]),
            ]
            for step, piece_ref in enumerate(pieces):
                first = tile * TILE_POINTS + lax.rem(mine + step, len(pieces)) * piece_rows
                first = pl.multiple_of(first, piece_rows)
                targets.append((pl.ds(first, piece_rows), piece_ref.at[which, :, cols]))
            for number, (taken, target) in enumerate(targets):
                done = left.at[which, start // PAIR, number]
                copy = pltpu.make_async_copy(sorted_kv.at[which, taken, cols], target, done)
                copy.start()
                leaving.append(copy)
    for copy in leaving:
        copy.wait()


def select_kernel(rule, lists_ref, got_ref, held_ref, out_ref):
    out_ref[...] = jnp.where(rule(lists_ref[0, 2 * BAND + 1]), got_ref[...], held_ref[...])


def place_kernel(order_ref, place_ref):
    place_ref[...] = place_rows(local_order(order_ref))


def query_kernel(order_ref, q_ref, qs_ref, pick):
    @pl.when(pl.program_id(0) == 0)
    def _():
        pick[...] = pick_rows(local_order(order_ref))

    qs_ref[...] = mm(pick[...], q_ref[...]).astype(jnp.bfloat16)


def own_kernel(lists_ref, qs_ref, kv_ref, acc_ref, ml_ref):
    count = qs_ref.shape[0]
    rows = bias_rows(lists_ref, count, count, 0, 0)
    heads = [columns_of(at) for at in range(PAIR_HEADS)]
    scores = [add_bias(mm_nt(kv_ref[0, :, cols], qs_ref[:, cols]), rows) for cols in heads]
    peaks = [peak_of(each) for each in scores]
    weights = [exp_of(each, peak) for each, peak in zip(scores, peaks)]
    ml_ref[...] = jnp.concatenate(peaks + [total_of(each) for each in weights], axis=0)
    for cols, each in zip(heads, weights):
        acc_ref[cols] = mm_tn(kv_ref[1, :, cols], each.astype(jnp.bfloat16))


def halo_place(is_low, count):
    tiles = count // TILE_POINTS
    start = pl.multiple_of(jnp.where(is_low, 0, count - HALO), HALO)
    return start, jnp.where(is_low, 0, tiles - BAND), jnp.where(is_low, -BAND, tiles)


def take_keys(ml, scores, values, summed):
    old = [ml[at : at + 1] for at in range(2 * PAIR_HEADS)]
    peaks = [jnp.maximum(was, peak_of(each)) for was, each in zip(old, scores)]
    weights = [exp_of(each, peak) for each, peak in zip(scores, peaks)]
    shrinks = [exp_of(was, peak) for was, peak in zip(old, peaks)]
    products = [mm_tn(value, each.astype(jnp.bfloat16)) for value, each in zip(values, weights)]
    totals = [was * shrink + total_of(each) for was, shrink, each in zip(old[PAIR_HEADS:], shrinks, weights)]
    return peaks, totals, [was * shrink + new for was, shrink, new in zip(summed, shrinks, products)]


def near_kernel(lists_ref, qs_ref, near_kv, acc_ref, ml_ref, new_acc_ref, new_ml_ref):
    new_acc_ref[...] = acc_ref[...]
    new_ml_ref[...] = ml_ref[...]

    @pl.when(meets_early())
    def _():
        start, first_query, first_key = halo_place(jnp.logical_not(in_lower_half()), qs_ref.shape[0])
        met = pl.ds(start, HALO)
        rows = bias_rows(lists_ref, HALO, HALO, first_query, first_key)
        heads = [columns_of(at) for at in range(PAIR_HEADS)]
        scores = [add_bias(mm_nt(near_kv[0, :, cols], qs_ref[met, cols]), rows) for cols in heads]
        values = [near_kv[1, :, cols] for cols in heads]
        summed = [acc_ref[cols, met] for cols in heads]
        peaks, totals, summed = take_keys(ml_ref[:, met], scores, values, summed)
        for cols, each in zip(heads, summed):
            new_acc_ref[cols, met] = each
        new_ml_ref[:, met] = jnp.concatenate(peaks + totals, axis=0)


def global_kernel(lists_ref, qs_ref, acc_ref, ml_ref, *rest):
    pieces, (new_acc_ref, new_ml_ref) = rest[:-2], rest[-2:]
    heads = [columns_of(at) for at in range(PAIR_HEADS)]
    keys = [jnp.concatenate([ref[0, :, cols] for ref in pieces], axis=0) for cols in heads]
    values = [jnp.concatenate([ref[1, :, cols] for ref in pieces], axis=0) for cols in heads]
    scores = [mm_nt(each, qs_ref[:, cols]) for each, cols in zip(keys, heads)]
    summed = [acc_ref[cols] for cols in heads]
    peaks, totals, summed = take_keys(ml_ref[...], scores, values, summed)
    for cols, each in zip(heads, summed):
        new_acc_ref[cols] = each
    new_ml_ref[...] = jnp.concatenate(peaks + totals, axis=0)


def finish_kernel(lists_ref, place_ref, qs_ref, acc_ref, ml_ref, *rest):
    next_kv, second_kv, odd_kv, out_ref, attended, halos, arrived = rest
    count = qs_ref.shape[0]
    here, end = lax.axis_index("grp"), lax.axis_size("grp") - 1
    at_end = (here == 0) | (here == end)
    even_wrap = (lax.rem(lax.axis_index("blk"), 2) == 0) == (here == end)
    sources = (
        (jnp.logical_not(at_end), 0, next_kv),
        (at_end & even_wrap, 0, second_kv),
        (at_end & jnp.logical_not(even_wrap), 0, odd_kv),
        (jnp.logical_not(meets_early()), 1, second_kv),
    )
    step = pl.program_id(0)

    blocks = halos.shape[3] // PAIR

    def copies_of(side, source, block):
        cols = pl.ds(block * PAIR, PAIR)
        return [
            pltpu.make_async_copy(source.at[w, :, cols], halos.at[side, w, :, cols], arrived.at[side, w, block])
            for w in range(2)
        ]

    @pl.when(step == 0)
    def _():
        for block in range(blocks):
            for chosen, side, source in sources:

                @pl.when(chosen)
                def _():
                    for copy in copies_of(side, source, block):
                        copy.start()

    def wait_for(side):
        for block in range(blocks):
            for chosen, here_side, source in sources:
                if here_side == side:

                    @pl.when(chosen & (step == block))
                    def _():
                        for copy in copies_of(side, source, block):
                            copy.wait()

    def add_halo(side, is_low):
        start, first_query, first_key = halo_place(is_low, count)
        met = pl.ds(start, HALO)
        rows = bias_rows(lists_ref, HALO, HALO, first_query, first_key)
        heads = [columns_of(at) for at in range(PAIR_HEADS)]
        here_cols = [
            pl.ds(pl.multiple_of(step * PAIR + at * HEAD_WIDTH, HEAD_WIDTH), HEAD_WIDTH) for at in range(PAIR_HEADS)
        ]
        keys = [halos[side, 0, :, cols] for cols in here_cols]
        values = [halos[side, 1, :, cols] for cols in here_cols]
        scores = [add_bias(mm_nt(key, qs_ref[met, cols]), rows) for key, cols in zip(keys, heads)]
        summed = [acc_ref[cols, met] for cols in heads]
        _, totals, summed = take_keys(ml_ref[:, met], scores, values, summed)
        for cols, each, total in zip(heads, summed, totals):
            attended[cols, met] = (each / total).astype(jnp.bfloat16)

    wait_for(0)
    add_halo(0, in_lower_half())
    wait_for(1)

    @pl.when(jnp.logical_not(meets_early()))
    def _():
        add_halo(1, jnp.logical_not(in_lower_half()))

    @pl.when(meets_early())
    def _():
        start, _, _ = halo_place(jnp.logical_not(in_lower_half()), count)
        left = pl.ds(start, HALO)
        for at in range(PAIR_HEADS):
            cols = columns_of(at)
            total = ml_ref[PAIR_HEADS + at : PAIR_HEADS + at + 1, left]
            attended[cols, left] = (acc_ref[cols, left] / total).astype(jnp.bfloat16)

    out_ref[...] = mm_nt(place_ref[...], attended[...]).astype(jnp.bfloat16)


def join_kernel(first, second, joined):
    rows = first.shape[1]
    joined[:, :rows] = first[...]
    joined[:, rows:] = second[...]


SMEM = pl.BlockSpec(memory_space=pltpu.SMEM)
VMEM = pl.BlockSpec(memory_space=pltpu.VMEM)
HBM = pl.BlockSpec(memory_space=pltpu.HBM)
ANY = pl.BlockSpec(memory_space=pl.ANY)
SORT_LIMIT = VMEM_LIMIT
LONG = 20000000000


def column_block(*leading):
    zeros = (0,) * len(leading)
    return pl.BlockSpec((*leading, PAIR), lambda i: (*zeros, i))


def row_block(rows, width):
    return pl.BlockSpec((rows, width), lambda i: (i, 0))


def whole_block(*shape):
    return pl.BlockSpec(shape, lambda i: (0,) * len(shape))


def spread_rounds(axis):
    count = lax.axis_size(axis)
    middle = count // 2

    def round_of(pairs, low_end, high_start):
        (_, upper), (_, lower) = pairs

        def rule(root):
            at = lax.axis_index(axis)
            return ((at == upper) & (root < low_end)) | ((at == lower) & (root >= high_start))

        return pairs, rule

    rounds = []
    for i in range(middle - 1):
        rounds.append(round_of([(i, i + 1), (count - 1 - i, count - 2 - i)], i + 1, count - 1 - i))
    rounds.append(round_of([(middle - 1, middle), (middle, middle - 1)], middle, middle))
    for i in range(middle - 1, 0, -1):
        rounds.append(round_of([(count - 1 - i, count - i), (i, i - 1)], count - i, i))
    return rounds


def body(query_rows, key_rows, value_rows, tile_lists, hilbert_order):
    row_count, feature_count = query_rows.shape
    tiles_here = row_count // TILE_POINTS
    blk_count, grp_count = lax.axis_size("blk"), lax.axis_size("grp")
    part = blk_count // NG
    bf16 = functools.partial(jax.ShapeDtypeStruct, dtype=jnp.bfloat16)
    f32 = functools.partial(jax.ShapeDtypeStruct, dtype=jnp.float32)

    def in_hbm(*arrays):
        return [pltpu.with_memory_space_constraint(array, pltpu.HBM) for array in arrays]

    def call(kernel, name, ins, outs, out_shape, scratch=(), cost=None, grid=(), limit=VMEM_LIMIT):
        return pl.pallas_call(
            kernel,
            grid=grid,
            in_specs=ins,
            out_specs=outs,
            out_shape=out_shape,
            scratch_shapes=scratch,
            cost_estimate=cost,
            compiler_params=pltpu.CompilerParams(vmem_limit_bytes=limit),
            name=name,
        )

    order = hilbert_order.reshape(1, row_count)
    piece_rows = TILE_POINTS // part
    halo = bf16((2, HALO, feature_count))
    kv, outward, inward, first_out, second_out, *pieces = call(
        sort_kernel,
        "sort_keys_values",
        [HBM] * 4,
        [ANY] * (5 + part),
        [bf16((2, row_count, feature_count)), *[halo] * 4]
        + [bf16((2, piece_rows, feature_count))] * part,
        [
            pltpu.SMEM(tile_lists.shape, jnp.int32),
            pltpu.VMEM((1, row_count), jnp.int32),
            pltpu.VMEM((2, row_count, feature_count), jnp.bfloat16),
            pltpu.VMEM((2, row_count, feature_count), jnp.bfloat16),
            pltpu.SemaphoreType.DMA((2, tiles_here)),
            pltpu.SemaphoreType.DMA((2, feature_count // PAIR, 5 + part)),
            pltpu.SemaphoreType.DMA((2,)),
        ],
        limit=SORT_LIMIT,
    )(tile_lists, order, *in_hbm(key_rows, value_rows))

    def owner_of(tile_id):
        owner = lax.div(lax.rem(tile_id, tiles_here * blk_count * grp_count // NG), tiles_here)
        return lax.div(owner, grp_count), lax.rem(owner, grp_count)

    def select(rule, got, held, flops=1):
        return call(
            functools.partial(select_kernel, rule),
            "select_piece",
            [SMEM] + [VMEM] * 2,
            VMEM,
            bf16(held.shape),
            cost=pl.CostEstimate(flops=flops, bytes_accessed=flops, transcendentals=0),
        )(tile_lists, got, held)

    middle = grp_count // 2
    away = [(i, i - 1) for i in range(1, middle)] + [(i, i + 1) for i in range(middle, grp_count - 1)]
    towards = [(target, source) for source, target in away]
    across = [(middle - 1, middle), (middle, middle - 1)]

    def exchange(turn):
        links = []
        for run in range(blk_count):
            down = (run + turn) % 2 == 1
            links += [(run * grp_count + i, run * grp_count + j) for i, j in away + across if (j < i) == down]
        return links + wraps[0] if turn == 1 else links

    wraps = [[], []]
    for run in range(1, blk_count):
        first = run * grp_count
        wraps[(run + 1) % 2] += [(first - 1, first), (first, first - 1)]
    tie = lax.optimization_barrier
    rounds = spread_rounds("grp")
    inner = middle - 1
    listed = tile_lists[0, 2 * BAND + 1] >= 0

    def stage(run, *operands):
        shapes = jax.eval_shape(run, *operands)
        skip = lambda *_: jax.tree.map(lambda leaf: jnp.zeros(leaf.shape, leaf.dtype), shapes)
        return lax.cond(listed, run, skip, *operands)

    def relay(piece, some):
        for pairs, rule in some:
            piece = take(rule, lax.ppermute(piece, "grp", pairs), piece)
        return piece

    def take(rule, got, piece, **cost):
        return select(lambda tile_id: rule(owner_of(tile_id)[1]), got, piece, **cost)

    grid = (feature_count // PAIR,)
    idle = pl.CostEstimate(flops=1, bytes_accessed=1, transcendentals=0)
    busy = pl.CostEstimate(flops=LONG, bytes_accessed=LONG, transcendentals=0)
    queries_block = column_block(row_count)
    state_blocks = [row_block(PAIR, row_count), row_block(STATE_ROWS, row_count)]
    state_shapes = [f32((feature_count, row_count)), f32((grid[0] * STATE_ROWS, row_count))]
    inward_rounds, across_round, outward_rounds = rounds[:inner], rounds[inner], rounds[inner + 1 :]

    def inward_stage(piece):
        queries = call(
            query_kernel,
            "sort_queries",
            [whole_block(1, row_count), queries_block],
            queries_block,
            bf16((row_count, feature_count)),
            [pltpu.VMEM((row_count, row_count), jnp.bfloat16)],
            cost=busy,
            grid=grid,
        )(order, query_rows)
        return lax.ppermute(piece, "grp", inward_rounds[-1][0]), queries

    def across_stage(piece, kv, queries):
        own = call(
            own_kernel,
            "attend_own",
            [SMEM, queries_block, column_block(2, row_count)],
            state_blocks,
            state_shapes,
            cost=busy,
            grid=grid,
        )(tile_lists, queries, kv)
        return relay(piece, [across_round]), own

    def outward_stage(piece, outward, second_out, queries, own, near_kv):
        place = call(
            place_kernel, "place_rows", [VMEM], VMEM, bf16((row_count, row_count)), cost=busy
        )(order)
        place, second_out = tie((place, second_out))
        second_kv = lax.ppermute(second_out, ("blk", "grp"), exchange(1))
        own = call(
            near_kernel,
            "attend_near",
            [SMEM, queries_block, column_block(2, HALO)] + state_blocks,
            state_blocks,
            state_shapes,
            cost=busy,
            grid=grid,
        )(tile_lists, queries, near_kv, *own)
        piece = relay(piece, outward_rounds[:-1])
        got = lax.ppermute(piece, "grp", outward_rounds[-1][0])
        piece = take(outward_rounds[-1][1], got, piece, flops=LONG)
        states, odd_kv = stage(plane_stage, piece, outward, queries, own)
        return states, place, second_kv, odd_kv

    def plane_stage(piece, outward, queries, own):
        for step in range(2):
            turns = [1 if i % part % 2 == step else 2 for i in range(blk_count)]
            links = [(i, (i // part ^ turn) * part + i % part) for i, turn in enumerate(turns)]
            got = lax.ppermute(piece, "blk", links)
            if step == 1:
                got, outward = tie((got, outward))
                odd_kv = lax.ppermute(outward, ("blk", "grp"), wraps[1])
            rows = 2 * piece.shape[1]
            joined = bf16((2, rows, feature_count))
            cost = (idle, busy)[step]
            piece = call(join_kernel, "join_pieces", [VMEM] * 2, VMEM, joined, cost=cost)(piece, got)
        return stage(global_stage, piece, queries, own), odd_kv

    def global_stage(quarters, queries, own):
        pieces = [quarters]
        for step in range(1, part):
            pairs = [(i, i // part * part + (i + step) % part) for i in range(blk_count)]
            pieces.append(lax.ppermute(quarters, "blk", pairs))
        return call(
            global_kernel,
            "attend_global",
            [SMEM, queries_block] + state_blocks + [column_block(2, NG * piece_rows)] * part,
            state_blocks,
            state_shapes,
            cost=idle,
            grid=grid,
        )(tile_lists, queries, *own, *pieces)

    near_kv = lax.ppermute(first_out, ("blk", "grp"), exchange(0))
    piece = pieces[0]
    for step in range(1, part):
        pairs = [(i, i // part * part + (i + step) % part) for i in range(blk_count)]
        got = lax.ppermute(pieces[step], "blk", pairs)

        def from_owner(tile_id, step=step):
            return lax.rem(lax.axis_index("blk") + part - step, part) == owner_of(tile_id)[0]

        piece = select(from_owner, got, piece, flops=LONG)
    piece = relay(piece, inward_rounds[:-1])
    got, queries = stage(inward_stage, piece)
    got, inward = tie((got, inward))
    next_kv = lax.ppermute(inward, "grp", towards)
    piece = take(inward_rounds[-1][1], got, piece)
    piece, own = stage(across_stage, piece, kv, queries)
    piece, near_kv = tie((piece, near_kv))
    states, place, second_kv, odd_kv = stage(outward_stage, piece, outward, second_out, queries, own, near_kv)
    return call(
        finish_kernel,
        "attend_last",
        [SMEM, whole_block(row_count, row_count), queries_block] + state_blocks + [ANY] * 3,
        queries_block,
        bf16((row_count, feature_count)),
        [
            pltpu.VMEM((PAIR, row_count), jnp.bfloat16),
            pltpu.VMEM((2, 2, HALO, feature_count), jnp.bfloat16),
            pltpu.SemaphoreType.DMA((2, 2, grid[0])),
        ],
        grid=grid,
    )(tile_lists, place, queries, *states, next_kv, second_kv, odd_kv)


def solution(mesh):
    rows = P(("blk", "grp"), None)
    in_specs = (rows, rows, rows, rows, P(("blk", "grp")))
    return jax.shard_map(body, mesh=mesh, in_specs=in_specs, out_specs=rows, check_vma=False)
```

```python
import functools

import jax
import jax.numpy as jnp
from jax import lax
from jax.experimental import pallas as pl
from jax.experimental.pallas import tpu as pltpu
from jax.sharding import PartitionSpec as P

LOCAL_HEADS = 8
HEAD_WIDTH = 128
TILE_POINTS = 128
BAND = 2
NG = 4
HALO = BAND * TILE_POINTS
PAIR_HEADS = 4
PAIR = PAIR_HEADS * HEAD_WIDTH
STATE_ROWS = 2 * PAIR_HEADS
MASKED = -1e30
EXP_SCALE = HEAD_WIDTH ** (-0.5) * 1.4426950408889634
VMEM_LIMIT = 16 * 1024 * 1024


def mm(a, b):
    return lax.dot_general(a, b, (((1,), (0,)), ((), ())), preferred_element_type=jnp.float32)


def mm_tn(a, b):
    return lax.dot_general(a, b, (((0,), (0,)), ((), ())), preferred_element_type=jnp.float32)


def mm_nt(a, b):
    return lax.dot_general(a, b, (((1,), (1,)), ((), ())), preferred_element_type=jnp.float32)


def pick_rows(order):
    count = order.shape[1]
    column = jnp.transpose(jnp.broadcast_to(order, (128, count)))
    lane = lax.broadcasted_iota(jnp.int32, (count, 128), 1)
    parts = [column == lane + start for start in range(0, count, 128)]
    return jnp.concatenate([p.astype(jnp.float32) for p in parts], axis=1).astype(jnp.bfloat16)


def place_rows(order):
    count = order.shape[1]
    row = lax.broadcasted_iota(jnp.int32, (count, count), 0)
    return (row == order).astype(jnp.float32).astype(jnp.bfloat16)


def local_order(order_ref):
    return jnp.bitwise_and(order_ref[...], order_ref.shape[1] - 1)


def bias_rows(lists_ref, queries, keys, first_query, first_key):
    rows = []
    for at in range(keys // TILE_POINTS):
        bias = []
        for query in range(queries // TILE_POINTS):
            slot = first_key + at - first_query - query + BAND
            listed = lists_ref[first_query + query, jnp.clip(slot, 0, 2 * BAND)] >= 0
            admitted = listed & (slot >= 0) & (slot <= 2 * BAND)
            value = jnp.where(admitted, 0.0, MASKED).astype(jnp.float32)
            bias.append(jnp.full((1, TILE_POINTS), value, jnp.float32))
        rows.append(jnp.concatenate(bias, axis=1))
    return rows


def add_bias(scores, rows):
    tiles = [scores[at * TILE_POINTS : (at + 1) * TILE_POINTS] + row for at, row in enumerate(rows)]
    return jnp.concatenate(tiles, axis=0)


def exp_of(scores, peak):
    return jnp.exp2((scores - peak) * EXP_SCALE)


def peak_of(scores):
    return jnp.max(scores, axis=0, keepdims=True)


def total_of(weights):
    return jnp.sum(weights, axis=0, keepdims=True)


def columns_of(head):
    return slice(head * HEAD_WIDTH, (head + 1) * HEAD_WIDTH)


def in_lower_half():
    return lax.axis_index("grp") < lax.axis_size("grp") // 2


def at_middle():
    here, middle = lax.axis_index("grp"), lax.axis_size("grp") // 2
    return (here == middle) | (here == middle - 1)


def meets_early():
    return in_lower_half() == (lax.rem(lax.axis_index("blk"), 2) == 1)


def sort_kernel(lists_hbm, order_hbm, k_hbm, v_hbm, kv_hbm, outward, inward, first_out, second_out, *rest):
    pieces = rest[:-7]
    lists_ref, order_ref, unsorted, sorted_kv, arrived, left, small = rest[-7:]
    count, width = k_hbm.shape
    order_copy = pltpu.make_async_copy(order_hbm, order_ref, small.at[0])
    lists_copy = pltpu.make_async_copy(lists_hbm, lists_ref, small.at[1])
    order_copy.start()
    lists_copy.start()
    copies = []
    for which, ref in enumerate((k_hbm, v_hbm)):
        for start in range(0, count, TILE_POINTS):
            rows = pl.ds(start, TILE_POINTS)
            done = arrived.at[which, start // TILE_POINTS]
            copies.append(pltpu.make_async_copy(ref.at[rows], unsorted.at[which, rows], done))
    for copy in copies:
        copy.start()
    order_copy.wait()
    pick = pick_rows(local_order(order_ref))
    lists_copy.wait()
    tile = lax.rem(lists_ref[0, 2 * BAND + 1], count // TILE_POINTS)
    mine = lax.rem(lax.axis_index("blk"), len(pieces))
    piece_rows = TILE_POINTS // len(pieces)
    low, high = 0, count - HALO
    out_start = jnp.where(in_lower_half(), low, high)
    in_start = jnp.where(in_lower_half(), high, low)
    first_start = jnp.where(at_middle() & jnp.logical_not(meets_early()), in_start, out_start)
    second_start = jnp.where(at_middle() & meets_early(), in_start, out_start)
    starts = (out_start, in_start, first_start, second_start)
    out_rows, in_rows, first_rows, second_rows = [pl.ds(pl.multiple_of(start, HALO), HALO) for start in starts]
    leaving = []
    for which in range(2):
        for copy in copies[which * len(copies) // 2 : (which + 1) * len(copies) // 2]:
            copy.wait()
        for start in range(0, width, PAIR):
            cols = pl.ds(start, PAIR)
            rows = mm(pick, unsorted[which, :, start : start + PAIR]).astype(jnp.bfloat16)
            sorted_kv[which, :, start : start + PAIR] = rows
            targets = [
                (slice(None), kv_hbm.at[which, :, cols]),
                (out_rows, outward.at[which, :, cols]),
                (in_rows, inward.at[which, :, cols]),
                (first_rows, first_out.at[which, :, cols]),
                (second_rows, second_out.at[which, :, cols]),
            ]
            for step, piece_ref in enumerate(pieces):
                first = tile * TILE_POINTS + lax.rem(mine + step, len(pieces)) * piece_rows
                first = pl.multiple_of(first, piece_rows)
                targets.append((pl.ds(first, piece_rows), piece_ref.at[which, :, cols]))
            for number, (taken, target) in enumerate(targets):
                done = left.at[which, start // PAIR, number]
                copy = pltpu.make_async_copy(sorted_kv.at[which, taken, cols], target, done)
                copy.start()
                leaving.append(copy)
    for copy in leaving:
        copy.wait()


def select_kernel(rule, lists_ref, got_ref, held_ref, out_ref):
    out_ref[...] = jnp.where(rule(lists_ref[0, 2 * BAND + 1]), got_ref[...], held_ref[...])


def query_kernel(order_ref, q_ref, qs_ref, pick):
    @pl.when(pl.program_id(0) == 0)
    def _():
        pick[...] = pick_rows(local_order(order_ref))

    qs_ref[...] = mm(pick[...], q_ref[...]).astype(jnp.bfloat16)


def own_kernel(lists_ref, qs_ref, kv_ref, acc_ref, ml_ref):
    count = qs_ref.shape[0]
    rows = bias_rows(lists_ref, count, count, 0, 0)
    heads = [columns_of(at) for at in range(PAIR_HEADS)]
    scores = [add_bias(mm_nt(kv_ref[0, :, cols], qs_ref[:, cols]), rows) for cols in heads]
    peaks = [peak_of(each) for each in scores]
    weights = [exp_of(each, peak) for each, peak in zip(scores, peaks)]
    ml_ref[...] = jnp.concatenate(peaks + [total_of(each) for each in weights], axis=0)
    for cols, each in zip(heads, weights):
        acc_ref[cols] = mm_tn(kv_ref[1, :, cols], each.astype(jnp.bfloat16))


def halo_place(is_low, count):
    tiles = count // TILE_POINTS
    start = pl.multiple_of(jnp.where(is_low, 0, count - HALO), HALO)
    return start, jnp.where(is_low, 0, tiles - BAND), jnp.where(is_low, -BAND, tiles)


def take_keys(ml, scores, values, summed):
    old = [ml[at : at + 1] for at in range(2 * PAIR_HEADS)]
    peaks = [jnp.maximum(was, peak_of(each)) for was, each in zip(old, scores)]
    weights = [exp_of(each, peak) for each, peak in zip(scores, peaks)]
    shrinks = [exp_of(was, peak) for was, peak in zip(old, peaks)]
    products = [mm_tn(value, each.astype(jnp.bfloat16)) for value, each in zip(values, weights)]
    totals = [was * shrink + total_of(each) for was, shrink, each in zip(old[PAIR_HEADS:], shrinks, weights)]
    return peaks, totals, [was * shrink + new for was, shrink, new in zip(summed, shrinks, products)]


def near_kernel(lists_ref, qs_ref, near_kv, acc_ref, ml_ref, new_acc_ref, new_ml_ref):
    new_acc_ref[...] = acc_ref[...]
    new_ml_ref[...] = ml_ref[...]

    @pl.when(meets_early())
    def _():
        start, first_query, first_key = halo_place(jnp.logical_not(in_lower_half()), qs_ref.shape[0])
        met = pl.ds(start, HALO)
        rows = bias_rows(lists_ref, HALO, HALO, first_query, first_key)
        heads = [columns_of(at) for at in range(PAIR_HEADS)]
        scores = [add_bias(mm_nt(near_kv[0, :, cols], qs_ref[met, cols]), rows) for cols in heads]
        values = [near_kv[1, :, cols] for cols in heads]
        summed = [acc_ref[cols, met] for cols in heads]
        peaks, totals, summed = take_keys(ml_ref[:, met], scores, values, summed)
        for cols, each in zip(heads, summed):
            new_acc_ref[cols, met] = each
        new_ml_ref[:, met] = jnp.concatenate(peaks + totals, axis=0)


def global_kernel(lists_ref, qs_ref, acc_ref, ml_ref, *rest):
    pieces, (new_acc_ref, new_ml_ref) = rest[:-2], rest[-2:]
    heads = [columns_of(at) for at in range(PAIR_HEADS)]
    keys = [jnp.concatenate([ref[0, :, cols] for ref in pieces], axis=0) for cols in heads]
    values = [jnp.concatenate([ref[1, :, cols] for ref in pieces], axis=0) for cols in heads]
    scores = [mm_nt(each, qs_ref[:, cols]) for each, cols in zip(keys, heads)]
    summed = [acc_ref[cols] for cols in heads]
    peaks, totals, summed = take_keys(ml_ref[...], scores, values, summed)
    for cols, each in zip(heads, summed):
        new_acc_ref[cols] = each
    new_ml_ref[...] = jnp.concatenate(peaks + totals, axis=0)


def finish_kernel(lists_ref, order_ref, qs_ref, acc_ref, ml_ref, *rest):
    next_kv, second_kv, odd_kv, out_ref, attended, halos, place, arrived = rest
    count = qs_ref.shape[0]
    here, end = lax.axis_index("grp"), lax.axis_size("grp") - 1
    at_end = (here == 0) | (here == end)
    even_wrap = (lax.rem(lax.axis_index("blk"), 2) == 0) == (here == end)
    sources = (
        (jnp.logical_not(at_end), 0, next_kv),
        (at_end & even_wrap, 0, second_kv),
        (at_end & jnp.logical_not(even_wrap), 0, odd_kv),
        (jnp.logical_not(meets_early()), 1, second_kv),
    )
    step = pl.program_id(0)

    blocks = halos.shape[3] // PAIR

    def copies_of(side, source, block):
        cols = pl.ds(block * PAIR, PAIR)
        return [
            pltpu.make_async_copy(source.at[w, :, cols], halos.at[side, w, :, cols], arrived.at[side, w, block])
            for w in range(2)
        ]

    @pl.when(step == 0)
    def _():
        for block in range(blocks):
            for chosen, side, source in sources:

                @pl.when(chosen)
                def _():
                    for copy in copies_of(side, source, block):
                        copy.start()

        place[...] = place_rows(local_order(order_ref))

    def wait_for(side):
        for block in range(blocks):
            for chosen, here_side, source in sources:
                if here_side == side:

                    @pl.when(chosen & (step == block))
                    def _():
                        for copy in copies_of(side, source, block):
                            copy.wait()

    def add_halo(side, is_low):
        start, first_query, first_key = halo_place(is_low, count)
        met = pl.ds(start, HALO)
        rows = bias_rows(lists_ref, HALO, HALO, first_query, first_key)
        heads = [columns_of(at) for at in range(PAIR_HEADS)]
        here_cols = [
            pl.ds(pl.multiple_of(step * PAIR + at * HEAD_WIDTH, HEAD_WIDTH), HEAD_WIDTH) for at in range(PAIR_HEADS)
        ]
        keys = [halos[side, 0, :, cols] for cols in here_cols]
        values = [halos[side, 1, :, cols] for cols in here_cols]
        scores = [add_bias(mm_nt(key, qs_ref[met, cols]), rows) for key, cols in zip(keys, heads)]
        summed = [acc_ref[cols, met] for cols in heads]
        _, totals, summed = take_keys(ml_ref[:, met], scores, values, summed)
        for cols, each, total in zip(heads, summed, totals):
            attended[cols, met] = (each / total).astype(jnp.bfloat16)

    wait_for(0)
    add_halo(0, in_lower_half())
    wait_for(1)

    @pl.when(jnp.logical_not(meets_early()))
    def _():
        add_halo(1, jnp.logical_not(in_lower_half()))

    @pl.when(meets_early())
    def _():
        start, _, _ = halo_place(jnp.logical_not(in_lower_half()), count)
        left = pl.ds(start, HALO)
        for at in range(PAIR_HEADS):
            cols = columns_of(at)
            total = ml_ref[PAIR_HEADS + at : PAIR_HEADS + at + 1, left]
            attended[cols, left] = (acc_ref[cols, left] / total).astype(jnp.bfloat16)

    out_ref[...] = mm_nt(place[...], attended[...]).astype(jnp.bfloat16)


def join_kernel(first, second, joined):
    rows = first.shape[1]
    joined[:, :rows] = first[...]
    joined[:, rows:] = second[...]


SMEM = pl.BlockSpec(memory_space=pltpu.SMEM)
VMEM = pl.BlockSpec(memory_space=pltpu.VMEM)
HBM = pl.BlockSpec(memory_space=pltpu.HBM)
ANY = pl.BlockSpec(memory_space=pl.ANY)
SORT_LIMIT = VMEM_LIMIT
LONG = 20000000000


def column_block(*leading):
    zeros = (0,) * len(leading)
    return pl.BlockSpec((*leading, PAIR), lambda i: (*zeros, i))


def row_block(rows, width):
    return pl.BlockSpec((rows, width), lambda i: (i, 0))


def whole_block(*shape):
    return pl.BlockSpec(shape, lambda i: (0,) * len(shape))


def spread_rounds(axis):
    count = lax.axis_size(axis)
    middle = count // 2

    def round_of(pairs, low_end, high_start):
        (_, upper), (_, lower) = pairs

        def rule(root):
            at = lax.axis_index(axis)
            return ((at == upper) & (root < low_end)) | ((at == lower) & (root >= high_start))

        return pairs, rule

    rounds = []
    for i in range(middle - 1):
        rounds.append(round_of([(i, i + 1), (count - 1 - i, count - 2 - i)], i + 1, count - 1 - i))
    rounds.append(round_of([(middle - 1, middle), (middle, middle - 1)], middle, middle))
    for i in range(middle - 1, 0, -1):
        rounds.append(round_of([(count - 1 - i, count - i), (i, i - 1)], count - i, i))
    return rounds


def body(query_rows, key_rows, value_rows, tile_lists, hilbert_order):
    row_count, feature_count = query_rows.shape
    tiles_here = row_count // TILE_POINTS
    blk_count, grp_count = lax.axis_size("blk"), lax.axis_size("grp")
    part = blk_count // NG
    bf16 = functools.partial(jax.ShapeDtypeStruct, dtype=jnp.bfloat16)
    f32 = functools.partial(jax.ShapeDtypeStruct, dtype=jnp.float32)

    def in_hbm(*arrays):
        return [pltpu.with_memory_space_constraint(array, pltpu.HBM) for array in arrays]

    def call(kernel, name, ins, outs, out_shape, scratch=(), cost=None, grid=(), limit=VMEM_LIMIT):
        return pl.pallas_call(
            kernel,
            grid=grid,
            in_specs=ins,
            out_specs=outs,
            out_shape=out_shape,
            scratch_shapes=scratch,
            cost_estimate=cost,
            compiler_params=pltpu.CompilerParams(vmem_limit_bytes=limit),
            name=name,
        )

    order = hilbert_order.reshape(1, row_count)
    piece_rows = TILE_POINTS // part
    halo = bf16((2, HALO, feature_count))
    kv, outward, inward, first_out, second_out, *pieces = call(
        sort_kernel,
        "sort_keys_values",
        [HBM] * 4,
        [ANY] * (5 + part),
        [bf16((2, row_count, feature_count)), *[halo] * 4]
        + [bf16((2, piece_rows, feature_count))] * part,
        [
            pltpu.SMEM(tile_lists.shape, jnp.int32),
            pltpu.VMEM((1, row_count), jnp.int32),
            pltpu.VMEM((2, row_count, feature_count), jnp.bfloat16),
            pltpu.VMEM((2, row_count, feature_count), jnp.bfloat16),
            pltpu.SemaphoreType.DMA((2, tiles_here)),
            pltpu.SemaphoreType.DMA((2, feature_count // PAIR, 5 + part)),
            pltpu.SemaphoreType.DMA((2,)),
        ],
        limit=SORT_LIMIT,
    )(tile_lists, order, *in_hbm(key_rows, value_rows))

    def owner_of(tile_id):
        owner = lax.div(lax.rem(tile_id, tiles_here * blk_count * grp_count // NG), tiles_here)
        return lax.div(owner, grp_count), lax.rem(owner, grp_count)

    def select(rule, got, held, flops=1):
        return call(
            functools.partial(select_kernel, rule),
            "select_piece",
            [SMEM] + [VMEM] * 2,
            VMEM,
            bf16(held.shape),
            cost=pl.CostEstimate(flops=flops, bytes_accessed=flops, transcendentals=0),
        )(tile_lists, got, held)

    middle = grp_count // 2
    away = [(i, i - 1) for i in range(1, middle)] + [(i, i + 1) for i in range(middle, grp_count - 1)]
    towards = [(target, source) for source, target in away]
    across = [(middle - 1, middle), (middle, middle - 1)]

    def exchange(turn):
        links = []
        for run in range(blk_count):
            down = (run + turn) % 2 == 1
            links += [(run * grp_count + i, run * grp_count + j) for i, j in away + across if (j < i) == down]
        return links + wraps[0] if turn == 1 else links

    wraps = [[], []]
    for run in range(1, blk_count):
        first = run * grp_count
        wraps[(run + 1) % 2] += [(first - 1, first), (first, first - 1)]
    tie = lax.optimization_barrier
    rounds = spread_rounds("grp")
    inner = middle - 1
    listed = tile_lists[0, 2 * BAND + 1] >= 0

    def stage(run, *operands):
        shapes = jax.eval_shape(run, *operands)
        skip = lambda *_: jax.tree.map(lambda leaf: jnp.zeros(leaf.shape, leaf.dtype), shapes)
        return lax.cond(listed, run, skip, *operands)

    def relay(piece, some):
        for pairs, rule in some:
            piece = take(rule, lax.ppermute(piece, "grp", pairs), piece)
        return piece

    def take(rule, got, piece, **cost):
        return select(lambda tile_id: rule(owner_of(tile_id)[1]), got, piece, **cost)

    grid = (feature_count // PAIR,)
    idle = pl.CostEstimate(flops=1, bytes_accessed=1, transcendentals=0)
    busy = pl.CostEstimate(flops=LONG, bytes_accessed=LONG, transcendentals=0)
    queries_block = column_block(row_count)
    state_blocks = [row_block(PAIR, row_count), row_block(STATE_ROWS, row_count)]
    state_shapes = [f32((feature_count, row_count)), f32((grid[0] * STATE_ROWS, row_count))]
    inward_rounds, across_round, outward_rounds = rounds[:inner], rounds[inner], rounds[inner + 1 :]

    def inward_stage(piece):
        queries = call(
            query_kernel,
            "sort_queries",
            [whole_block(1, row_count), queries_block],
            queries_block,
            bf16((row_count, feature_count)),
            [pltpu.VMEM((row_count, row_count), jnp.bfloat16)],
            cost=busy,
            grid=grid,
        )(order, query_rows)
        return lax.ppermute(piece, "grp", inward_rounds[-1][0]), queries

    def across_stage(piece, kv, queries):
        own = call(
            own_kernel,
            "attend_own",
            [SMEM, queries_block, column_block(2, row_count)],
            state_blocks,
            state_shapes,
            cost=busy,
            grid=grid,
        )(tile_lists, queries, kv)
        return relay(piece, [across_round]), own

    def outward_stage(piece, outward, second_out, queries, own, near_kv):
        second_kv = lax.ppermute(second_out, ("blk", "grp"), exchange(1))
        own = call(
            near_kernel,
            "attend_near",
            [SMEM, queries_block, column_block(2, HALO)] + state_blocks,
            state_blocks,
            state_shapes,
            cost=busy,
            grid=grid,
        )(tile_lists, queries, near_kv, *own)
        piece = relay(piece, outward_rounds[:-1])
        got = lax.ppermute(piece, "grp", outward_rounds[-1][0])
        piece = take(outward_rounds[-1][1], got, piece, flops=LONG)
        states, odd_kv = stage(plane_stage, piece, outward, queries, own)
        return states, second_kv, odd_kv

    def plane_stage(piece, outward, queries, own):
        for step in range(2):
            turns = [1 if i % part % 2 == step else 2 for i in range(blk_count)]
            links = [(i, (i // part ^ turn) * part + i % part) for i, turn in enumerate(turns)]
            got = lax.ppermute(piece, "blk", links)
            if step == 1:
                got, outward = tie((got, outward))
                odd_kv = lax.ppermute(outward, ("blk", "grp"), wraps[1])
            rows = 2 * piece.shape[1]
            joined = bf16((2, rows, feature_count))
            cost = (idle, busy)[step]
            piece = call(join_kernel, "join_pieces", [VMEM] * 2, VMEM, joined, cost=cost)(piece, got)
        return stage(global_stage, piece, queries, own), odd_kv

    def global_stage(quarters, queries, own):
        pieces = [quarters]
        for step in range(1, part):
            pairs = [(i, i // part * part + (i + step) % part) for i in range(blk_count)]
            pieces.append(lax.ppermute(quarters, "blk", pairs))
        return call(
            global_kernel,
            "attend_global",
            [SMEM, queries_block] + state_blocks + [column_block(2, NG * piece_rows)] * part,
            state_blocks,
            state_shapes,
            cost=idle,
            grid=grid,
        )(tile_lists, queries, *own, *pieces)

    near_kv = lax.ppermute(first_out, ("blk", "grp"), exchange(0))
    piece = pieces[0]
    for step in range(1, part):
        pairs = [(i, i // part * part + (i + step) % part) for i in range(blk_count)]
        got = lax.ppermute(pieces[step], "blk", pairs)

        def from_owner(tile_id, step=step):
            return lax.rem(lax.axis_index("blk") + part - step, part) == owner_of(tile_id)[0]

        piece = select(from_owner, got, piece, flops=LONG)
    piece = relay(piece, inward_rounds[:-1])
    got, queries = stage(inward_stage, piece)
    got, inward = tie((got, inward))
    next_kv = lax.ppermute(inward, "grp", towards)
    piece = take(inward_rounds[-1][1], got, piece)
    piece, own = stage(across_stage, piece, kv, queries)
    piece, near_kv = tie((piece, near_kv))
    states, second_kv, odd_kv = stage(outward_stage, piece, outward, second_out, queries, own, near_kv)
    return call(
        finish_kernel,
        "attend_last",
        [SMEM, whole_block(1, row_count), queries_block] + state_blocks + [ANY] * 3,
        queries_block,
        bf16((row_count, feature_count)),
        [
            pltpu.VMEM((PAIR, row_count), jnp.bfloat16),
            pltpu.VMEM((2, 2, HALO, feature_count), jnp.bfloat16),
            pltpu.VMEM((row_count, row_count), jnp.bfloat16),
            pltpu.SemaphoreType.DMA((2, 2, grid[0])),
        ],
        grid=grid,
    )(tile_lists, order, queries, *states, next_kv, second_kv, odd_kv)


def solution(mesh):
    rows = P(("blk", "grp"), None)
    in_specs = (rows, rows, rows, rows, P(("blk", "grp")))
    return jax.shard_map(body, mesh=mesh, in_specs=in_specs, out_specs=rows, check_vma=False)
```
